256 devices in a mesh: expert: 64 (over y, z, core), row: 4 (over x).
Axes of the slice: x: 4, y: 4, z: 8, core: 2. Of those that a mesh axis runs over, the one named last changes fastest.
Arguments:
- tokens: bfloat16 [1024, 7168], P('expert', 'row'), may hold values from -6 to 6
- routes: int32 [1024, 8], P('expert'), may hold values from 0 to 63, all different within a row; in each aligned block of 16 rows (0 to 15, 16 to 31, ...) at most 4 rows name the same one
- probs: float32 [1024, 8], P('expert'), may hold values from 0.02 to 0.3
- gate_weight: bfloat16 [64, 1024, 7168], P('expert', 'row'), may hold values from -0.0625 to 0.0625
- up_weight: bfloat16 [64, 1024, 7168], P('expert', 'row'), may hold values from -0.0625 to 0.0625
- down_weight: bfloat16 [64, 1024, 7168], P('expert', 'row'), may hold values from -0.1875 to 0.1875
- masks: int32 [64, 1024, 128], P('expert', 'row'), may hold values from 0 to 1, as said below
- inv_factor: float32 [128, 128], replicated, as said below
Outputs:
- pruned_panel: bfloat16 [64, 1024, 128], P('expert', 'row')
- moe_out: bfloat16 [1024, 7168], P('expert', 'row')
- hessian: float32 [7168, 7168], P('row', 'expert')
The draws below stay inside these ranges and needn't reach their ends.
Inputs may be any that keep to these rules, and one draw needn't show every extreme that they name: `routes`: a token's 8 entries name different experts; within the rows of one device (aligned blocks of 16 tokens) no expert is named more than 4 times, a bound that some block reaches. `masks`: in each aligned group of 4 columns of a row exactly 2 entries are 1. `inv_factor`: upper triangular with a positive diagonal.
All inputs are finite; a program needn't handle non-finite values.
Results may differ from the reference program's by a relative error of at most 0.0075.
Values may be sent and summed in bfloat16 or wider, within the bound.
A program may use at most 128 MiB of HBM per device.

```python
import math
import jax
import jax.numpy as jnp
import numpy as np
from jax import lax

D = 7168
FF = 1024
PANEL = 128
TOP = 8
TOK_DEV = 16
EXPERTS = 64
TOKENS = 1024
CAP = 4
N_EXPERT = 64


def draw_masks(key, part):
    key = jax.random.fold_in(key, 11)
    pattern = jax.random.randint(key, (EXPERTS, FF, PANEL // 4), 0, 6)
    table = jnp.array([[1, 1, 0, 0], [1, 0, 1, 0], [1, 0, 0, 1], [0, 1, 1, 0], [0, 1, 0, 1], [0, 0, 1, 1]], jnp.int32)
    picked = jnp.zeros((EXPERTS, FF, PANEL // 4, 4), jnp.int32)
    for option in range(6):
        picked = picked + jnp.where(pattern[..., None] == option, table[option][None, None, None, :], 0)
    return picked.reshape(EXPERTS, FF, PANEL).astype(jnp.int32)


def draw_inv_factor(key, part):
    key = jax.random.fold_in(key, 17)
    first_key, second_key = jax.random.split(key)
    diagonal = jax.random.uniform(first_key, (PANEL,), jnp.float32, 1.0, 2.0)
    spread = jax.random.normal(second_key, (PANEL, PANEL), jnp.float32) * 0.5
    spread = spread / jnp.sqrt(jnp.float32(PANEL))
    index = jnp.arange(PANEL)
    upper = index[:, None] < index[None, :]
    eye_mask = index[:, None] == index[None, :]
    return jnp.where(upper, spread, 0.0) + jnp.where(eye_mask, diagonal[None, :], 0.0)


def steps_of(rng, shape, cuts, least, largest):
    loudness = 1.0
    for axis_at, parts in cuts:
        heights = jax.random.uniform(jax.random.fold_in(jax.random.fold_in(rng, 6), axis_at), (parts,), jnp.float32, least / len(cuts), largest / len(cuts))
        loudness = loudness * jnp.repeat(jnp.exp(heights), shape[axis_at] // parts).reshape((-1,) + (1,) * (len(shape) - 1 - axis_at))
    return loudness


def shared_out(stream_key, own, number, rows, number_of, top, reach, skew):
    order = jax.random.permutation(stream_key, number_of)
    heavy_load, ordinary = shares(number_of, rows * top, reach, skew, True), shares(number_of, rows * top, reach, skew, False)
    places = jnp.arange(number_of)

    def named(sizes, turn):
        used = int((sizes > 0).sum())
        fixed = max(1, used // 4)
        shifted = fixed + (places - fixed + turn * (used - fixed)) % max(1, number_of - fixed)
        return jnp.zeros((number_of,), jnp.int32).at[order[jnp.where(places < fixed, places, shifted)]].set(jnp.asarray(sizes, jnp.int32))

    sizes = jnp.where(number % 4 == 0, named(heavy_load, number // 4), named(ordinary, number - number // 4 - 1))
    mixed = jax.random.permutation(jax.random.fold_in(own, 3), number_of)
    giver, taker = mixed[0:number_of // 2 * 2:2], mixed[1:number_of // 2 * 2:2]
    room = jnp.minimum(sizes[giver] - 1, reach - sizes[taker]) // 2
    room = jnp.where((giver == order[0]) | (taker == order[0]) | (sizes[taker] == 0), 0, jnp.maximum(room, 0))
    shifted = jax.random.randint(jax.random.fold_in(own, 4), (number_of // 2,), 0, 1 << 20) % (room + 1)
    sizes = sizes.at[giver].add(-shifted).at[taker].add(shifted)
    labels = jnp.searchsorted(jnp.cumsum(sizes), jnp.arange(rows * top), side="right").astype(jnp.int32)
    listing = labels.reshape(top, rows).T
    listing = listing[jax.random.permutation(jax.random.fold_in(own, 1), rows)]
    turn = jax.random.randint(jax.random.fold_in(own, 2), (rows, 1), 0, top)
    return jnp.take_along_axis(listing, (jnp.arange(top)[None, :] + turn) % top, axis=1)


def shares(amount, total, most, skew, full):
    portions = [(1 << 20) // math.isqrt(standing ** skew) + 1 for standing in range(1, amount + 1)]
    largest = most if full else min(most, max(-(-total // amount), total * portions[0] // sum(portions)))
    least = 1 if total - largest >= amount - 1 else 0
    given, spare = [largest] + [least] * (amount - 1), total - largest - least * (amount - 1)
    while spare > 0:
        movable = [i for i in range(1, amount) if given[i] < largest] or [i for i in range(1, amount) if given[i] < most]
        whole, left = sum([portions[i] for i in movable]), spare
        for i in movable:
            more = min(most - given[i], max(1, left * portions[i] // whole), spare)
            given[i] = given[i] + more
            spare = spare - more
    return np.array(given)


def bell_draw(rng, dims, deviation, most, cuts=(), kind=jnp.bfloat16):
    factor_of = steps_of(rng, dims, cuts, -0.22, 0.18) if cuts else 1.0
    entries = jax.random.normal(rng, dims, jnp.float32) * deviation * factor_of
    return jnp.minimum(jnp.maximum(entries, -most), most).astype(kind)


def setup_inputs(seed: int = 0) -> dict:
    seeds = jax.random.split(jax.random.key(seed), 9)
    tokens = bell_draw(seeds[0], (TOKENS, D), 1.0, 6.0, ((0, 64), (1, 4)))
    routes_keys = jax.random.split(jax.random.fold_in(seeds[1], 1), TOKENS // TOK_DEV)
    routes_turns = jax.random.permutation(jax.random.fold_in(seeds[1], 3), TOKENS // TOK_DEV)
    routes = jax.vmap(lambda own, number: shared_out(jax.random.fold_in(seeds[1], 2), own, number, TOK_DEV, EXPERTS, TOP, CAP, 2))(routes_keys, routes_turns).reshape((TOKENS, TOP))
    probs = jnp.clip(0.02 + 0.28 * jax.random.uniform(seeds[2], (TOKENS, TOP), jnp.float32) ** steps_of(seeds[2], (TOKENS, TOP), ((0, 64),), -0.2, 0.2), 0.02, 0.3)
    gate_weight = bell_draw(seeds[3], (EXPERTS, FF, D), D ** -0.5, 0.0625, ((0, 64), (1, 4)))
    up_weight = bell_draw(seeds[4], (EXPERTS, FF, D), D ** -0.5, 0.0625, ((0, 64), (1, 4)))
    down_weight = bell_draw(seeds[5], (EXPERTS, FF, D), FF ** -0.5, 0.1875, ((0, 64), (1, 4)))
    masks = draw_masks(jax.random.fold_in(seeds[8], 71), 0)
    inv_factor = draw_inv_factor(jax.random.fold_in(seeds[8], 71), 0)
    return dict(tokens=tokens, routes=routes, probs=probs, gate_weight=gate_weight, up_weight=up_weight, down_weight=down_weight, masks=masks, inv_factor=inv_factor)


def prune_panel(gate_weight, masks, inv_factor):
    current = gate_weight[:, :, D - PANEL:].astype(jnp.float32)
    keep_mask = masks.astype(jnp.float32)
    columns = jnp.arange(PANEL, dtype=jnp.int32)

    def column_step(column_idx, current):
        column = lax.dynamic_index_in_dim(current, column_idx, 2, keepdims=False)
        keep_col = lax.dynamic_index_in_dim(keep_mask, column_idx, 2, keepdims=False)
        kept_vals = column * keep_col
        factor_row = lax.dynamic_index_in_dim(inv_factor, column_idx, 0, keepdims=False)
        errors_now = (column - kept_vals) / factor_row[column_idx]
        current = current - errors_now[:, :, None] * factor_row[None, None, :]
        return jnp.where(columns == column_idx, kept_vals[:, :, None], current)

    return lax.fori_loop(0, PANEL, column_step, current).astype(jnp.bfloat16)


def reference(tokens, routes, probs, gate_weight, up_weight, down_weight, masks, inv_factor):
    pruned = prune_panel(gate_weight, masks, inv_factor)
    gate_full = jnp.concatenate([gate_weight[:, :, :D - PANEL], pruned], axis=2)
    limit = N_EXPERT * CAP
    positions = jnp.arange(TOKENS, dtype=jnp.int32)
    contract = (((1,), (1,)), ((), ()))

    def expert_step(total, expert_id):
        hits = routes == expert_id
        share = jnp.sum(jnp.where(hits, probs, jnp.float32(0.0)), axis=1)
        routed = jnp.any(hits, axis=1)
        order = jnp.argsort(jnp.where(routed, 0, 1).astype(jnp.int32) * TOKENS + positions)[:limit].astype(jnp.int32)
        chosen = tokens[order]
        gate_val = lax.dot_general(chosen, gate_full[expert_id], contract, preferred_element_type=jnp.float32)
        up_val = lax.dot_general(chosen, up_weight[expert_id], contract, preferred_element_type=jnp.float32)
        hidden = (jax.nn.silu(gate_val) * up_val).astype(jnp.bfloat16)
        output = jnp.dot(hidden, down_weight[expert_id], preferred_element_type=jnp.float32).astype(jnp.bfloat16)
        weight_rows = jnp.where(routed[order], share[order], jnp.float32(0.0))
        return total.at[order].add(weight_rows[:, None] * output.astype(jnp.float32)), None

    total, unused = lax.scan(expert_step, jnp.zeros((TOKENS, D), jnp.float32), jnp.arange(EXPERTS, dtype=jnp.int32))
    moe_out = total.astype(jnp.bfloat16)
    hessian = (2.0 / TOKENS) * jnp.dot(moe_out.T, moe_out, preferred_element_type=jnp.float32)
    return pruned, moe_out, hessian
```

```python
import functools

import jax
import jax.numpy as jnp
from jax import lax
from jax.experimental import pallas as pl
from jax.experimental.pallas import tpu as pltpu
from jax.sharding import PartitionSpec as P

NX, NY, NZ, NC = 4, 4, 8, 2
TOK = 16
CAP = 4
PANEL = 128
FB = 1792
WA = 1024
WB = FB - WA
INFO = 128
SLOTS = CAP * NY * NZ * NC
CH = SLOTS // NY
HID = 256
CT = NZ * NC * TOK
BLK = 112
MESH = pl.DeviceIdType.MESH
F32 = jnp.float32
BF = jnp.bfloat16
COPIES = 160


def wrap(value, n):
    return lax.rem(value + 4 * n, n)


def iota(shape, axis):
    return lax.broadcasted_iota(jnp.int32, shape, axis)


def interleave(*gens):
    gens = list(gens)
    while gens:
        for gen in list(gens):
            try:
                next(gen)
            except StopIteration:
                gens.remove(gen)


class Net:
    def __init__(self, send, recv):
        self.send, self.recv, self.count, self.pending = send, recv, 0, []

    def copy(self, src, dst, dev):
        index = self.count
        self.count += 1
        made = pltpu.make_async_remote_copy(
            src_ref=src,
            dst_ref=dst,
            send_sem=self.send.at[index],
            recv_sem=self.recv.at[index],
            device_id=dev,
            device_id_type=MESH,
        )
        made.start()
        self.pending.append(made)
        return made

    def drain(self):
        for made in self.pending:
            made.wait_send()


def ring_gather(net, n, me, d, slot, dev, got):
    half = n // 2
    forward = net.copy(slot(me), slot(me), dev(wrap(me + d, n)))
    backward = net.copy(slot(me), slot(me), dev(wrap(me - d, n)))
    yield
    for step in range(1, half + 1):
        origin = wrap(me - d * step, n)
        forward.wait_recv()
        if step < half:
            forward = net.copy(slot(origin), slot(origin), dev(wrap(me + d, n)))
        got(origin)
        if step < half:
            other = wrap(me + d * step, n)
            backward.wait_recv()
            if step < half - 1:
                backward = net.copy(slot(other), slot(other), dev(wrap(me - d, n)))
            got(other)
        yield


def ring_scatter(net, n, me, d, mine, dev, stage, land, done):
    half = n // 2

    def send(hop, value, target):
        stage.at[hop][...] = value.astype(BF)
        return net.copy(stage.at[hop], land.at[hop], dev(wrap(target, n)))

    forward = send(0, mine(wrap(me + d * half, n)), me + d)
    backward = send(half, mine(wrap(me - d * (half - 1), n)), me - d)
    yield
    for step in range(2, half + 1):
        forward.wait_recv()
        value = land[step - 2].astype(F32) + mine(wrap(me + d * (half + 1 - step), n))
        forward = send(step - 1, value, me + d)
        if step < half:
            backward.wait_recv()
            value = land[half + step - 2].astype(F32) + mine(wrap(me - d * (half - step), n))
            backward = send(half + step - 1, value, me - d)
        yield
    own = mine(me)
    backward.wait_recv()
    own = own + land[2 * half - 2].astype(F32)
    forward.wait_recv()
    done(own + land[half - 1].astype(F32))
    yield


def body(
    tokens, routes, probs, gate, up, down, masks, factor,
    pruned_out, moe_out, hess_out,
    gate_v, up_v, down_v, ga, gb, rows, sel, slot_prob, part, xstage, xland,
    ca, cb, sa, sb, ra, rb, ya_s, ya_l, za_s, za_l, yb_s, yb_l, zb_s, zb_l,
    la, lb, right, w_t, drop_t, v_t, err_t, wsem, send, recv,
):
    expert = lax.axis_index("expert")
    x = lax.axis_index("row")
    y, z, c = expert // (NZ * NC), (expert // NC) % NZ, expert % NC
    d = 1 - 2 * c
    net = Net(send, recv)

    def at_y(i):
        return ((i * NZ + z) * NC + c, x)

    def at_z(i):
        return ((y * NZ + i) * NC + c, x)

    def at_x(i):
        return (expert, i)

    sibling = (expert + d, x)

    weights = {}
    for number, (src, dst) in enumerate(((gate, gate_v), (up, up_v), (down, down_v))):
        for part_idx in range(NX):
            weights[number, part_idx] = pltpu.make_async_copy(
                src.at[:, pl.ds(part_idx * FB, FB)], dst.at[part_idx], wsem.at[number * NX + part_idx]
            )
    for key in ((0, 3), (0, 0), (0, 1), (0, 2), (1, 0), (1, 1), (1, 2), (1, 3), (2, 0), (2, 1), (2, 2), (2, 3)):
        weights[key].start()

    barrier = pltpu.get_barrier_semaphore()
    near = [sibling]
    near += [at_y(wrap(y + 1, NY)), at_y(wrap(y - 1, NY))]
    near += [at_z(wrap(z + 1, NZ)), at_z(wrap(z - 1, NZ))]
    near += [at_x(wrap(x + k, NX)) for k in (1, 2, 3)]
    for device in near:
        pl.semaphore_signal(barrier, inc=1, device_id=device, device_id_type=MESH)

    lane = iota((TOK, INFO), 1)
    dense = jnp.zeros((TOK, INFO), F32)
    for k in range(routes.shape[1]):
        dense = dense + jnp.where(routes[:, k : k + 1] == lane % 64, probs[:, k : k + 1], 0.0)
    high = dense.astype(BF).astype(F32)
    info = jnp.where(lane < 64, high, dense - high).astype(BF)
    ga[y, z, c] = tokens[:, :WA]
    gb[y, z, c, :, :WB] = tokens[:, WA:]
    gb[y, z, c, :, WB:] = info

    pl.semaphore_wait(barrier, len(near))

    def gather(a_ref, b_ref):
        shared = []

        def share(ref):
            shared.append(net.copy(ref, ref, sibling))

        def skip(origin):
            pass

        def chain_a():
            yield from ring_gather(net, NZ, z, d, lambda i: a_ref.at[y, i, c], at_z, skip)
            share(a_ref.at[y, :, c])
            yield from ring_gather(
                net, NY, y, d, lambda i: a_ref.at[i, :, c], at_y, lambda i: share(a_ref.at[i, :, c])
            )

        def chain_b():
            yield from ring_gather(net, NY, y, d, lambda i: b_ref.at[i, z, c], at_y, skip)
            share(b_ref.at[:, z, c])
            yield from ring_gather(
                net, NZ, z, d, lambda i: b_ref.at[:, i, c], at_z, lambda i: share(b_ref.at[:, i, c])
            )

        return chain_a, chain_b, shared

    def prune():
        weights[0, 3].wait()
        w_t[...] = gate_v[3, :, FB - PANEL :].astype(F32).T
        drop_t[...] = (1 - masks[...]).astype(F32).T
        eye = iota((PANEL, PANEL), 0) == iota((PANEL, PANEL), 1)
        upper = factor[...]
        diagonal = jnp.sum(jnp.where(eye, upper, 0.0), axis=1, keepdims=True)
        v_t[...] = (upper / diagonal).T
        err_t[...] = jnp.zeros_like(err_t)
        yield
        for block in range(PANEL // 16):
            lo, hi = block * 16, block * 16 + 16
            seg = w_t[lo:hi, :]
            if block:
                seg = seg - jnp.dot(
                    v_t[lo:hi, :], err_t[...], precision=lax.Precision.HIGHEST, preferred_element_type=F32
                )
            near_t = v_t[lo:hi, lo:hi]
            drop = drop_t[lo:hi, :]
            errors = []
            for i in range(16):
                error = seg[i : i + 1, :] * drop[i : i + 1, :]
                errors.append(error)
                seg = seg - near_t[:, i : i + 1] * error
            err_t[lo:hi, :] = jnp.concatenate(errors, axis=0)
            w_t[lo:hi, :] = seg * (1.0 - drop)
            yield
        result = w_t[...].T.astype(BF)
        pruned_out[...] = result
        gate_v[3, :, FB - PANEL :] = result

    chain_a, chain_b, shared = gather(ga, gb)
    interleave(chain_a(), chain_b(), prune())
    for made in shared:
        made.wait_recv()

    pick = iota((8, INFO), 1)
    pick = jnp.where((pick == expert) | (pick == expert + 64), 1.0, 0.0).astype(BF)
    before = (iota((CT, CT), 0) // TOK == iota((CT, CT), 1) // TOK) & (iota((CT, CT), 0) < iota((CT, CT), 1))
    before = before.astype(F32).astype(BF)
    slot_i, tok_i = iota((CH, CT), 0), iota((CH, CT), 1)
    ring_x = {}
    for k in range(NY):
        j = k
        prob = lax.dot_general(
            pick,
            gb[j, :, :, :, WB:].reshape(CT, INFO),
            (((1,), (1,)), ((), ())),
            preferred_element_type=F32,
        )
        hit = prob > 0.0
        rank = jnp.dot(hit.astype(F32).astype(BF), before, preferred_element_type=F32)
        chosen = (
            (slot_i // CAP == tok_i // TOK)
            & (rank[0:1, :] == (slot_i % CAP).astype(F32))
            & (prob[0:1, :] > 0.0)
        )
        chosen_f = jnp.where(chosen, 1.0, 0.0)
        slot_prob[j] = jnp.sum(chosen_f * prob[0:1, :], axis=1, keepdims=True)
        sel[j] = chosen_f
        chosen_b = chosen_f.astype(BF)
        rows[x, j, :, :WA] = jnp.dot(chosen_b, ga[j].reshape(CT, WA), preferred_element_type=F32).astype(BF)
        rows[x, j, :, WA:] = jnp.dot(
            chosen_b, gb[j, :, :, :, :WB].reshape(CT, WB), preferred_element_type=F32
        ).astype(BF)
        gen = ring_gather(net, NX, x, d, lambda i, j=j: rows.at[i, j], at_x, lambda i: None)
        next(gen)
        ring_x[k] = gen

    for key in sorted(weights):
        if key != (0, 3):
            weights[key].wait()

    contract = (((1,), (1,)), ((), ()))

    def project(o):
        block = rows[o].reshape(SLOTS, FB)
        return (
            lax.dot_general(block, gate_v[o], contract, preferred_element_type=F32),
            lax.dot_general(block, up_v[o], contract, preferred_element_type=F32),
        )

    gate_val, up_val = project(x)
    for k in range(NY):
        next(ring_x[k])
    for o in (wrap(x - d, NX), wrap(x + d, NX)):
        more = project(o)
        gate_val, up_val = gate_val + more[0], up_val + more[1]
    for k in range(NY):
        interleave(ring_x[k])
    more = project(wrap(x + 2, NX))
    gate_val, up_val = gate_val + more[0], up_val + more[1]
    hidden = (gate_val / (1.0 + jnp.exp(-gate_val)) * up_val).astype(BF)

    def partial(o):
        part[o] = (
            jnp.dot(hidden, down_v[o], preferred_element_type=F32).astype(BF).reshape(NY, CH, FB)
        )

    share_a, share_b = {}, {}

    def finish(j):
        def run(total):
            scaled = (total * slot_prob[j]).astype(BF)
            back = sel[j].T.astype(BF)
            spread = jnp.dot(back, scaled, preferred_element_type=F32).astype(BF)
            ca[j] = spread[:, :WA].reshape(NZ, NC, TOK, WA)
            cb[j] = spread[:, WA:].reshape(NZ, NC, TOK, WB)
            share_a[j] = net.copy(ca.at[j, :, 1 - c], sa.at[j], sibling)
            share_b[j] = net.copy(cb.at[j, :, 1 - c], sb.at[j], sibling)

        return run

    for o in (wrap(x + 2, NX), wrap(x - d, NX), wrap(x + d, NX), x):
        partial(o)
    gens = []
    for j in range(NY):
        gens.append(
            ring_scatter(
                net, NX, x, d, lambda i, j=j: part[i, j].astype(F32), at_x, xstage.at[j], xland.at[j], finish(j)
            )
        )
    interleave(*gens)
    for j in range(NY):
        share_a[j].wait_recv()
        share_b[j].wait_recv()

    chain_la, chain_lb, shared = gather(la, lb)

    def return_a():
        def hold(value):
            ra[...] = value

        def final(value):
            value = value.astype(BF)
            moe_out[:, :WA] = value
            la[y, z, c] = value

        yield from ring_scatter(
            net, NY, y, d, lambda i: ca[i, :, c].astype(F32) + sa[i].astype(F32), at_y, ya_s, ya_l, hold
        )
        yield from ring_scatter(net, NZ, z, d, lambda i: ra[i], at_z, za_s, za_l, final)
        yield from chain_la()

    def return_b():
        def hold(value):
            rb[...] = value

        def final(value):
            value = value.astype(BF)
            moe_out[:, WA:] = value
            lb[y, z, c] = value

        yield from ring_scatter(
            net, NZ, z, d, lambda i: cb[:, i, c].astype(F32) + sb[:, i].astype(F32), at_z, zb_s, zb_l, hold
        )
        yield from ring_scatter(net, NY, y, d, lambda i: rb[i], at_y, yb_s, yb_l, final)
        yield from chain_lb()

    interleave(return_a(), return_b())
    for made in shared:
        made.wait_recv()

    first = net.count
    copies = [
        pltpu.make_async_remote_copy(
            src_ref=right,
            dst_ref=right,
            send_sem=send.at[first + k],
            recv_sem=recv.at[first],
            device_id=at_x(wrap(x + 1 + k, NX)),
            device_id_type=MESH,
        )
        for k in range(NX - 1)
    ]

    @pl.when(x == y)
    def _():
        offset = (z * NC + c) * BLK
        at = iota((PANEL, FB), 1) - offset
        unit = jnp.where((at == iota((PANEL, FB), 0)) & (at < BLK), 1.0, 0.0).astype(BF)
        for j in range(NY):
            picked = lax.dot_general(
                unit[:, :WA], la[j].reshape(CT, WA), contract, preferred_element_type=F32
            ) + lax.dot_general(unit[:, WA:], lb[j].reshape(CT, WB), contract, preferred_element_type=F32)
            right[:, j * CT : (j + 1) * CT] = picked.astype(BF)
        for made in copies:
            made.start()
        for made in copies:
            made.wait_send()

    @pl.when(x != y)
    def _():
        copies[0].wait_recv()

    scale = 2.0 / (TOK * NY * NZ * NC)
    for ref, base, width in ((la, 0, WA), (lb, WA, WB)):
        for col in range(0, width, 256):
            total = jnp.zeros((PANEL, 256), F32)
            for j in range(NY):
                total = total + jnp.dot(
                    right[:, j * CT : (j + 1) * CT],
                    ref[j, :, :, :, col : col + 256].reshape(CT, 256),
                    preferred_element_type=F32,
                )
            hess_out[base + col : base + col + 256, :] = (total * scale).T[:, :BLK]
    net.drain()


def on_device(tokens, routes, probs, gate_weight, up_weight, down_weight, masks, inv_factor):
    vmem = pl.BlockSpec(memory_space=pltpu.VMEM)
    hbm = pl.BlockSpec(memory_space=pl.ANY)
    scratch = [
        pltpu.VMEM((NX, HID, FB), BF),
        pltpu.VMEM((NX, HID, FB), BF),
        pltpu.VMEM((NX, HID, FB), BF),
        pltpu.VMEM((NY, NZ, NC, TOK, WA), BF),
        pltpu.VMEM((NY, NZ, NC, TOK, WB + INFO), BF),
        pltpu.VMEM((NX, NY, CH, FB), BF),
        pltpu.VMEM((NY, CH, CT), F32),
        pltpu.VMEM((NY, CH, 1), F32),
        pltpu.VMEM((NX, NY, CH, FB), BF),
        pltpu.VMEM((NY, 3, CH, FB), BF),
        pltpu.VMEM((NY, 3, CH, FB), BF),
        pltpu.VMEM((NY, NZ, NC, TOK, WA), BF),
        pltpu.VMEM((NY, NZ, NC, TOK, WB), BF),
        pltpu.VMEM((NY, NZ, TOK, WA), BF),
        pltpu.VMEM((NY, NZ, TOK, WB), BF),
        pltpu.VMEM((NZ, TOK, WA), F32),
        pltpu.VMEM((NY, TOK, WB), F32),
        pltpu.VMEM((3, NZ, TOK, WA), BF),
        pltpu.VMEM((3, NZ, TOK, WA), BF),
        pltpu.VMEM((7, TOK, WA), BF),
        pltpu.VMEM((7, TOK, WA), BF),
        pltpu.VMEM((3, TOK, WB), BF),
        pltpu.VMEM((3, TOK, WB), BF),
        pltpu.VMEM((7, NY, TOK, WB), BF),
        pltpu.VMEM((7, NY, TOK, WB), BF),
        pltpu.VMEM((NY, NZ, NC, TOK, WA), BF),
        pltpu.VMEM((NY, NZ, NC, TOK, WB), BF),
        pltpu.VMEM((PANEL, NY * CT), BF),
        pltpu.VMEM((PANEL, HID), F32),
        pltpu.VMEM((PANEL, HID), F32),
        pltpu.VMEM((PANEL, PANEL), F32),
        pltpu.VMEM((PANEL, HID), F32),
        pltpu.SemaphoreType.DMA((12,)),
        pltpu.SemaphoreType.DMA((COPIES,)),
        pltpu.SemaphoreType.DMA((COPIES,)),
    ]
    pruned, moe, hessian = pl.pallas_call(
        body,
        out_shape=(
            jax.ShapeDtypeStruct((HID, PANEL), BF),
            jax.ShapeDtypeStruct((TOK, FB), BF),
            jax.ShapeDtypeStruct((FB, BLK), F32),
        ),
        in_specs=[vmem, vmem, vmem, hbm, hbm, hbm, vmem, vmem],
        out_specs=(vmem, vmem, vmem),
        scratch_shapes=scratch,
        compiler_params=pltpu.CompilerParams(
            collective_id=0, has_side_effects=True, vmem_limit_bytes=58 * 1024 * 1024
        ),
        cost_estimate=pl.CostEstimate(flops=6_000_000_000, bytes_accessed=14_000_000, transcendentals=65536),
        name="expert_layer",
    )(tokens, routes, probs, gate_weight[0], up_weight[0], down_weight[0], masks[0], inv_factor)
    return pruned[None], moe, hessian


def solution(mesh):
    in_specs = (
        P("expert", "row"),
        P("expert", None),
        P("expert", None),
        P("expert", "row", None),
        P("expert", "row", None),
        P("expert", "row", None),
        P("expert", "row", None),
        P(),
    )
    out_specs = (P("expert", "row", None), P("expert", "row"), P("row", "expert"))
    return jax.shard_map(
        on_device, mesh=mesh, in_specs=in_specs, out_specs=out_specs, check_vma=False
    )
```

```python
import functools

import jax
import jax.numpy as jnp
from jax import lax
from jax.experimental import pallas as pl
from jax.experimental.pallas import tpu as pltpu
from jax.sharding import PartitionSpec as P

NX, NY, NZ, NC = 4, 4, 8, 2
TOK = 16
CAP = 4
PANEL = 128
FB = 1792
HALF = FB // 2
INFO = 128
WIDE = INFO + FB
CUTS = ((0, INFO + HALF), (INFO + HALF, HALF))
RET = (1024, FB - 1024)
BASE = (0, RET[0])
WB = 256
WA = RET[1] - WB
SLOTS = CAP * NY * NZ * NC
CH = SLOTS // NY
HID = 256
CT = NZ * NC * TOK
BLK = 112
MESH = pl.DeviceIdType.MESH
F32 = jnp.float32
BF = jnp.bfloat16
COPIES = 240
CONTRACT = (((1,), (1,)), ((), ()))
ZNEAR = (1, 7, 2, 6, 3, 5, 4)
YNEAR = (1, 3)
PLANES = (0, 1, 3, 2)


def wrap(value, n):
    return lax.rem(value + 4 * n, n)


def iota(shape, axis):
    return lax.broadcasted_iota(jnp.int32, shape, axis)


class Net:
    def __init__(self, send, recv):
        self.send, self.recv, self.count, self.pending = send, recv, 0, []

    def make(self, src, dst, dev, recv_index=None):
        index = self.count
        self.count += 1
        return pltpu.make_async_remote_copy(
            src_ref=src,
            dst_ref=dst,
            send_sem=self.send.at[index],
            recv_sem=self.recv.at[index if recv_index is None else recv_index],
            device_id=dev,
            device_id_type=MESH,
        )

    def copy(self, src, dst, dev):
        made = self.make(src, dst, dev)
        made.start()
        self.pending.append(made)
        return made

    def drain(self):
        for made in self.pending:
            made.wait_send()


def body(
    tokens, routes, probs, gate, up, down, masks, factor,
    pruned_out, moe_out, hess_out,
    gate_v, up_v, down_v, got, rows, sel, slot_prob, part, turn, land,
    spread, sib, ysend, yland, own, zsend, zland,
    full, unit, right, acc, w_t, drop_t, v_t, err_t, wsem, send, recv,
):
    expert = lax.axis_index("expert")
    x = lax.axis_index("row")
    y, z, c = expert // (NZ * NC), (expert // NC) % NZ, expert % NC
    d = 1 - 2 * c
    net = Net(send, recv)

    def at_y(k):
        return ((wrap(y + k, NY) * NZ + z) * NC + c, x)

    def at_z(k):
        return ((y * NZ + wrap(z + k, NZ)) * NC + c, x)

    def at_x(k):
        return (expert, wrap(x + k, NX))

    sibling = (expert + d, x)

    barrier = pltpu.get_barrier_semaphore()
    near = [sibling]
    near += [at_y(k) for k in range(1, NY)]
    near += [at_z(k) for k in range(1, NZ)]
    near += [at_x(k) for k in range(1, NX)]
    for device in near:
        pl.semaphore_signal(barrier, inc=1, device_id=device, device_id_type=MESH)

    weights = {}
    for number, (src, dst) in enumerate(((gate, gate_v), (up, up_v), (down, down_v))):
        for at in (3, 0, 1, 2):
            made = pltpu.make_async_copy(
                src.at[:, pl.ds(at * FB, FB)], dst.at[at], wsem.at[number * NX + at]
            )
            made.start()
            weights[number, at] = made

    lane = iota((INFO, TOK), 0)
    dense = jnp.zeros((INFO, TOK), F32)
    for k in range(routes.shape[0]):
        dense = dense + jnp.where(routes[k : k + 1, :] == lane % 64, probs[k : k + 1, :], 0.0)
    high = dense.astype(BF).astype(F32)
    info = jnp.where(lane < 64, high, dense - high)
    got[y, z, c, :, :INFO] = info.T.astype(BF)
    got[y, z, c, :, INFO:] = tokens[...]

    pl.semaphore_wait(barrier, len(near))

    def prune():
        weights[0, 3].wait()
        w_t[...] = gate_v[3, :, FB - PANEL :].astype(F32).T
        drop_t[...] = (1 - masks[...]).astype(F32).T
        eye = iota((PANEL, PANEL), 0) == iota((PANEL, PANEL), 1)
        upper = factor[...]
        diagonal = jnp.sum(jnp.where(eye, upper, 0.0), axis=1, keepdims=True)
        v_t[...] = (upper / diagonal).T
        err_t[...] = jnp.zeros_like(err_t)
        yield
        for block in range(PANEL // 16):
            lo, hi = block * 16, block * 16 + 16
            seg = w_t[lo:hi, :]
            if block:
                seg = seg - jnp.dot(
                    v_t[lo:hi, :], err_t[...], precision=lax.Precision.HIGHEST, preferred_element_type=F32
                )
            near_t = v_t[lo:hi, lo:hi]
            drop = drop_t[lo:hi, :]
            errors = []
            for i in range(16):
                error = seg[i : i + 1, :] * drop[i : i + 1, :]
                errors.append(error)
                seg = seg - near_t[:, i : i + 1] * error
            err_t[lo:hi, :] = jnp.concatenate(errors, axis=0)
            w_t[lo:hi, :] = seg * (1.0 - drop)
            yield
        result = w_t[...].T.astype(BF)
        pruned_out[...] = result
        gate_v[3, :, FB - PANEL :] = result
        at = iota((PANEL, FB), 1) - (z * NC + c) * BLK
        unit[...] = jnp.where((at == iota((PANEL, FB), 0)) & (at < BLK), 1.0, 0.0).astype(BF)

    pruning = prune()

    def tick(times):
        for _ in range(times):
            next(pruning, None)

    def cut(ref, h):
        return ref.at[:, pl.ds(CUTS[h][0], CUTS[h][1])]

    along_z, along_y, shared = {}, {}, {}
    for h in range(2):
        block = cut(got.at[y, z, c], h)
        for k in ZNEAR:
            along_z[h, k] = net.copy(block, block, at_z(k))
        for m in YNEAR:
            along_y[h, 0, m] = net.copy(block, block, at_y(m))
    tick(3)

    before = (iota((CT, CT), 0) // TOK == iota((CT, CT), 1) // TOK) & (iota((CT, CT), 0) < iota((CT, CT), 1))
    before = before.astype(F32).astype(BF)
    slot_i, tok_i = iota((CH, CT), 0), iota((CH, CT), 1)
    pick = iota((8, INFO), 1)
    pick = jnp.where((pick == expert) | (pick == expert + 64), 1.0, 0.0).astype(BF)

    def choose(j):
        prob = lax.dot_general(
            pick, got[j, :, :, :, :INFO].reshape(CT, INFO), CONTRACT, preferred_element_type=F32
        )
        rank = jnp.dot((prob > 0.0).astype(F32).astype(BF), before, preferred_element_type=F32)
        chosen = (
            (slot_i // CAP == tok_i // TOK)
            & (rank[0:1, :] == (slot_i % CAP).astype(F32))
            & (prob[0:1, :] > 0.0)
        )
        chosen = jnp.where(chosen, 1.0, 0.0)
        slot_prob[j] = jnp.sum(chosen * prob[0:1, :], axis=1, keepdims=True)
        sel[j] = chosen

    ring = {}

    def launch(m, h):
        j = wrap(y - m, NY)
        shared[m, h].wait_recv()
        if h == 0:
            choose(j)
        start, width = CUTS[h][0] + (INFO if h == 0 else 0), HALF
        rows[x, h, j] = jnp.dot(
            sel[j].astype(BF),
            got[j, :, :, :, start : start + width].reshape(CT, width),
            preferred_element_type=F32,
        ).astype(BF)
        block = rows.at[x, h, j]
        ring[m, h, 0] = net.copy(block, block, at_x(d))
        ring[m, h, 1] = net.copy(block, block, at_x(-d))

    def relay(m, h):
        j = wrap(y - m, NY)
        ring[m, h, 0].wait_recv()
        block = rows.at[wrap(x - d, NX), h, j]
        ring[m, h, 2] = net.copy(block, block, at_x(d))

    def share(m, h):
        ref = got.at[wrap(y - m, NY), :, c, :, pl.ds(CUTS[h][0], CUTS[h][1])]
        shared[m, h] = net.copy(ref, ref, sibling)

    def forward(h, ks):
        for k in ks:
            along_z[h, k].wait_recv()
            block = cut(got.at[y, wrap(z - k, NZ), c], h)
            for m in YNEAR:
                along_y[h, k, m] = net.copy(block, block, at_y(m))

    def arrive(m, h):
        for k in (0,) + ZNEAR if m != 2 else (0,):
            along_y[h, k, m].wait_recv()
        if m == (1, 3)[h]:
            ref = got.at[wrap(y - m, NY), :, c, :, pl.ds(CUTS[h][0], CUTS[h][1])]
            along_y[h, 0, 2] = net.copy(ref, ref, at_y(m))
        share(m, h)

    forward(0, ZNEAR)
    share(0, 0)
    tick(1)
    forward(1, ZNEAR[:2])
    launch(0, 0)
    forward(1, ZNEAR[2:])
    share(0, 1)
    tick(1)
    launch(0, 1)
    relay(0, 0)
    order = [(0, 0), (0, 1), (1, 0), (3, 0), (3, 1), (1, 1), (2, 0), (2, 1)]
    arrive(*order[2])
    for n in range(2, len(order)):
        tick(1)
        if n < len(order) - 1:
            arrive(*order[n + 1])
        launch(*order[n])
        relay(*order[n - 1])
    relay(*order[-1])
    tick(16)

    for key in sorted(weights):
        if key != (0, 3):
            weights[key].wait()

    def project(o, h):
        block = rows[o, h].reshape(SLOTS, HALF)
        at = slice(h * HALF, (h + 1) * HALF)
        return (
            lax.dot_general(block, gate_v[o, :, at], CONTRACT, preferred_element_type=F32),
            lax.dot_general(block, up_v[o, :, at], CONTRACT, preferred_element_type=F32),
        )

    gate_val, up_val = project(x, 0)
    for hop, o in ((None, x), (1, wrap(x + d, NX)), (0, wrap(x - d, NX)), (2, wrap(x + 2, NX))):
        for h in range(2):
            if hop is None and h == 0:
                continue
            if hop in (1, 2):
                for m in PLANES:
                    ring[m, h, hop].wait_recv()
            more = project(o, h)
            gate_val, up_val = gate_val + more[0], up_val + more[1]
    hidden = (gate_val / (1.0 + jnp.exp(-gate_val)) * up_val).astype(BF)

    def partial(o):
        part[o] = jnp.dot(hidden, down_v[o], preferred_element_type=F32).astype(BF).reshape(NY, CH, FB)

    steps = (2, 1, 3, 0)
    planes = [wrap(y + k, NY) for k in steps]
    sums, back, along, across = {}, {}, {}, {}

    def place(n):
        h = n // NY
        return planes[n % NY], pl.ds(BASE[h], RET[h]), pl.ds(0, RET[h])

    def first(n):
        j, at, to = place(n)
        sums[n, 0] = net.copy(part.at[wrap(x + 2, NX), j, :, at], land.at[n, 0, :, to], at_x(d))

    def other(n):
        j, at, to = place(n)
        sums[n, 1] = net.copy(part.at[wrap(x - d, NX), j, :, at], land.at[n, 1, :, to], at_x(-d))

    def second(n):
        j, at, to = place(n)
        sums[n, 0].wait_recv()
        turn[n, :, to] = (land[n, 0, :, to].astype(F32) + part[wrap(x + d, NX), j, :, at].astype(F32)).astype(BF)
        sums[n, 2] = net.copy(turn.at[n, :, to], land.at[n, 2, :, to], at_x(d))

    def finish(n):
        j, at, to = place(n)
        sums[n, 1].wait_recv()
        sums[n, 2].wait_recv()
        total = part[x, j, :, at].astype(F32) + land[n, 1, :, to].astype(F32) + land[n, 2, :, to].astype(F32)
        scaled = (total * slot_prob[j]).astype(BF)
        spread[n, :, :, :, to] = (
            jnp.dot(sel[j].T.astype(BF), scaled, preferred_element_type=F32)
            .astype(BF)
            .reshape(NZ, NC, TOK, RET[n // NY])
        )
        back[n] = net.copy(spread.at[n, :, 1 - c, :, to], sib.at[n, :, :, to], sibling)

    def onward(n):
        back[n].wait_recv()
        h, k = n // NY, n % NY
        to = pl.ds(0, RET[h])
        total = spread[n, :, c, :, to].astype(F32) + sib[n, :, :, to].astype(F32)
        if k < NY - 1:
            slot = h * (NY - 1) + k
            ysend[slot, :, :, to] = total.astype(BF)
            along[h, k] = net.copy(ysend.at[slot, :, :, to], yland.at[slot, :, :, to], at_y(steps[k]))
        else:
            own[h, :, :, to] = total

    def whole(h, i):
        to = pl.ds(0, RET[h])
        total = own[h, i, :, to]
        for k in range(NY - 1):
            total = total + yland[h * (NY - 1) + k, i, :, to].astype(F32)
        return total

    def cross(h):
        for k in range(NY - 1):
            along[h, k].wait_recv()
        for k in ZNEAR:
            slot = h * (NZ - 1) + k - 1
            to = pl.ds(0, RET[h])
            zsend[slot, :, to] = whole(h, wrap(z + k, NZ)).astype(BF)
            across[h, k] = net.copy(zsend.at[slot, :, to], zland.at[slot, :, to], at_z(k))

    def settle(h):
        result = whole(h, z)
        for k in ZNEAR:
            across[h, k].wait_recv()
            result = result + zland[h * (NZ - 1) + k - 1, :, pl.ds(0, RET[h])].astype(F32)
        result = result.astype(BF)
        moe_out[:, pl.ds(BASE[h], RET[h])] = result
        full[y, z, c, :, pl.ds(BASE[h], RET[h])] = result

    cuts = (pl.ds(0, RET[0]), pl.ds(RET[0], WA))
    tail = pl.ds(RET[0] + WA, WB)
    az, ay, by, bz, sa = {}, {}, {}, {}, {}

    def spread_z(h):
        ref = full.at[y, z, c, :, cuts[h]]
        for k in ZNEAR:
            az[h, k] = net.copy(ref, ref, at_z(k))
        for m in YNEAR:
            ay[h, 0, m] = net.copy(ref, ref, at_y(m))

    def spread_y(h, ks):
        for k in ks:
            az[h, k].wait_recv()
            ref = full.at[y, wrap(z - k, NZ), c, :, cuts[h]]
            for m in YNEAR:
                ay[h, k, m] = net.copy(ref, ref, at_y(m))

    def draw(j, h):
        at = pl.ds(BASE[h], RET[h])
        more = lax.dot_general(
            unit[:, at], full[j, :, :, :, at].reshape(CT, RET[h]), CONTRACT, preferred_element_type=F32
        ).astype(BF)
        right[j] = more if h == 0 else right[j] + more

    def share_own(h):
        ref = full.at[y, :, c, :, cuts[h]]
        sa[h, 0] = net.copy(ref, ref, sibling)

    def collect(h, m):
        for k in (0,) + ZNEAR if m != 2 else (0,):
            ay[h, k, m].wait_recv()
        ref = full.at[wrap(y - m, NY), :, c, :, cuts[h]]
        if m == (1, 3)[h]:
            ay[h, 0, 2] = net.copy(ref, ref, at_y(m))
        sa[h, m] = net.copy(ref, ref, sibling)

    partial(wrap(x + 2, NX))
    for n in range(3):
        first(n)
    partial(wrap(x - d, NX))
    for n in range(3):
        other(n)
    partial(wrap(x + d, NX))
    partial(x)
    for n in range(2 * NY):
        second(n)
        if n + 3 < 2 * NY:
            first(n + 3)
            other(n + 3)
        if n >= 1:
            finish(n - 1)
        if n >= 2:
            onward(n - 2)
    cross(0)
    finish(7)
    onward(6)
    onward(7)
    settle(0)
    spread_z(0)
    cross(1)
    spread_y(0, ZNEAR)
    share_own(0)
    settle(1)
    ref = full.at[y, z, c, :, tail]
    for m in (1, 2, 3):
        by[m] = net.copy(ref, ref, at_y(m))
    spread_z(1)
    spread_y(1, ZNEAR[:2])
    for m in (1, 2, 3):
        by[m].wait_recv()
    ref = full.at[:, z, c, :, tail]
    for k in ZNEAR:
        bz[k] = net.copy(ref, ref, at_z(k))
    spread_y(1, ZNEAR[2:])
    share_own(1)
    for m in PLANES:
        if m:
            collect(0, m)
        sa[0, m].wait_recv()
        pl.when(x == y)(functools.partial(draw, wrap(y - m, NY), 0))
    for k in ZNEAR:
        bz[k].wait_recv()
    ref = full.at[:, :, c, :, tail]
    sb = net.copy(ref, ref, sibling)
    sb.wait_recv()

    scale = 2.0 / (TOK * NY * NZ * NC)
    cols = {}

    def product(n):
        j = wrap(y - PLANES[n], NY)

        @pl.when(x != y)
        def _():
            cols[n][0].wait_recv()

        for at in range(0, FB, 256):
            more = jnp.dot(
                right[j], full[j, :, :, :, at : at + 256].reshape(CT, 256), preferred_element_type=F32
            )
            if n == 0:
                acc[:, at : at + 256] = more
            elif n < NY - 1:
                acc[:, at : at + 256] += more
            else:
                hess_out[:, at : at + 256] = ((acc[:, at : at + 256] + more) * scale)[:BLK, :]

    for n, m in enumerate(PLANES):
        j = wrap(y - m, NY)
        if m:
            collect(1, m)
        sa[1, m].wait_recv()
        index = net.count
        cols[n] = [net.make(right.at[j], right.at[j], at_x(k), index) for k in (2, 1, 3)]

        @pl.when(x == y)
        def _():
            draw(j, 1)
            for made in cols[n]:
                made.start()

        if n:
            product(n - 1)
    product(NY - 1)

    @pl.when(x == y)
    def _():
        for n in range(NY):
            for made in cols[n]:
                made.wait_send()

    net.drain()


def hand_on(pruned, moe, hessian, pruned_out, moe_out, hess_out):
    pruned_out[...] = pruned[...]
    moe_out[...] = moe[...]
    hess_out[...] = hessian[...]


def on_device(tokens, routes, probs, gate_weight, up_weight, down_weight, masks, inv_factor):
    vmem = pl.BlockSpec(memory_space=pltpu.VMEM)
    hbm = pl.BlockSpec(memory_space=pl.ANY)
    scratch = [
        pltpu.VMEM((NX, HID, FB), BF),
        pltpu.VMEM((NX, HID, FB), BF),
        pltpu.VMEM((NX, HID, FB), BF),
        pltpu.VMEM((NY, NZ, NC, TOK, WIDE), BF),
        pltpu.VMEM((NX, 2, NY, CH, HALF), BF),
        pltpu.VMEM((NY, CH, CT), F32),
        pltpu.VMEM((NY, CH, 1), F32),
        pltpu.VMEM((NX, NY, CH, FB), BF),
        pltpu.VMEM((2 * NY, CH, RET[0]), BF),
        pltpu.VMEM((2 * NY, 3, CH, RET[0]), BF),
        pltpu.VMEM((2 * NY, NZ, NC, TOK, RET[0]), BF),
        pltpu.VMEM((2 * NY, NZ, TOK, RET[0]), BF),
        pltpu.VMEM((2 * NY - 2, NZ, TOK, RET[0]), BF),
        pltpu.VMEM((2 * NY - 2, NZ, TOK, RET[0]), BF),
        pltpu.VMEM((2, NZ, TOK, RET[0]), F32),
        pltpu.VMEM((2 * NZ - 2, TOK, RET[0]), BF),
        pltpu.VMEM((2 * NZ - 2, TOK, RET[0]), BF),
        pltpu.VMEM((NY, NZ, NC, TOK, FB), BF),
        pltpu.VMEM((PANEL, FB), BF),
        pltpu.VMEM((NY, PANEL, CT), BF),
        pltpu.VMEM((PANEL, FB), F32),
        pltpu.VMEM((PANEL, HID), F32),
        pltpu.VMEM((PANEL, HID), F32),
        pltpu.VMEM((PANEL, PANEL), F32),
        pltpu.VMEM((PANEL, HID), F32),
        pltpu.SemaphoreType.DMA((12,)),
        pltpu.SemaphoreType.DMA((COPIES,)),
        pltpu.SemaphoreType.DMA((COPIES,)),
    ]
    shapes = (
        jax.ShapeDtypeStruct((HID, PANEL), BF),
        jax.ShapeDtypeStruct((TOK, FB), BF),
        jax.ShapeDtypeStruct((BLK, FB), F32),
    )
    results = pl.pallas_call(
        body,
        out_shape=shapes,
        in_specs=[vmem, vmem, vmem, hbm, hbm, hbm, vmem, vmem],
        out_specs=(vmem, vmem, vmem),
        scratch_shapes=scratch,
        compiler_params=pltpu.CompilerParams(
            collective_id=0, has_side_effects=True, vmem_limit_bytes=58 * 1024 * 1024
        ),
        cost_estimate=pl.CostEstimate(flops=6_000_000_000, bytes_accessed=14_000_000, transcendentals=65536),
        name="expert_layer",
    )(tokens, routes.T, probs.T, gate_weight[0], up_weight[0], down_weight[0], masks[0], inv_factor)
    pruned, moe, hessian = pl.pallas_call(
        hand_on,
        out_shape=shapes,
        in_specs=[vmem, vmem, vmem],
        out_specs=(vmem, vmem, vmem),
        name="hand_on",
    )(*results)
    return pruned[None], moe, hessian.T


def solution(mesh):
    in_specs = (
        P("expert", "row"),
        P("expert", None),
        P("expert", None),
        P("expert", "row", None),
        P("expert", "row", None),
        P("expert", "row", None),
        P("expert", "row", None),
        P(),
    )
    out_specs = (P("expert", "row", None), P("expert", "row"), P("row", "expert"))
    return jax.shard_map(
        on_device, mesh=mesh, in_specs=in_specs, out_specs=out_specs, check_vma=False
    )
```

```python
import functools

import jax
import jax.numpy as jnp
from jax import lax
from jax.experimental import pallas as pl
from jax.experimental.pallas import tpu as pltpu
from jax.sharding import PartitionSpec as P

NX, NY, NZ, NC = 4, 4, 8, 2
TOK = 16
CAP = 4
PANEL = 128
FB = 1792
HALF = FB // 2
INFO = 128
WIDE = INFO + FB
CUTS = ((0, INFO + HALF), (INFO + HALF, HALF))
RET = (896, FB - 896)
BASE = (0, RET[0])
WB = 128
WA = RET[1] - WB
SLOTS = CAP * NY * NZ * NC
CH = SLOTS // NY
HID = 256
CT = NZ * NC * TOK
BLK = 112
MESH = pl.DeviceIdType.MESH
F32 = jnp.float32
BF = jnp.bfloat16
COPIES = 240
CONTRACT = (((1,), (1,)), ((), ()))
ZNEAR = (1, 7, 2, 6, 3, 5, 4)
YNEAR = (1, 3)
HOPS = ((1, 3, 2), (1, 3, 2))
PLANES = (0, 1, 3, 2)


def wrap(value, n):
    return lax.rem(value + 4 * n, n)


def iota(shape, axis):
    return lax.broadcasted_iota(jnp.int32, shape, axis)


class Net:
    def __init__(self, send, recv):
        self.send, self.recv, self.count, self.pending = send, recv, 0, []

    def make(self, src, dst, dev, recv_index=None):
        index = self.count
        self.count += 1
        return pltpu.make_async_remote_copy(
            src_ref=src,
            dst_ref=dst,
            send_sem=self.send.at[index],
            recv_sem=self.recv.at[index if recv_index is None else recv_index],
            device_id=dev,
            device_id_type=MESH,
        )

    def copy(self, src, dst, dev):
        made = self.make(src, dst, dev)
        made.start()
        self.pending.append(made)
        return made

    def drain(self):
        for made in self.pending:
            made.wait_send()


def body(
    tokens, routes, probs, gate, up, down, masks, factor,
    pruned_out, moe_out, hess_out,
    gate_v, up_v, down_v, got, rows, sel, slot_prob, part, turn, land,
    spread, sib, ysend, yland, own, zsend, zland,
    full, unit, right, acc, w_t, drop_t, v_t, err_t, wsem, send, recv,
):
    expert = lax.axis_index("expert")
    x = lax.axis_index("row")
    y, z, c = expert // (NZ * NC), (expert // NC) % NZ, expert % NC
    d = 1 - 2 * c
    net = Net(send, recv)

    def at_y(k):
        return ((wrap(y + k, NY) * NZ + z) * NC + c, x)

    def at_z(k):
        return ((y * NZ + wrap(z + k, NZ)) * NC + c, x)

    def at_x(k):
        return (expert, wrap(x + k, NX))

    sibling = (expert + d, x)

    barrier = pltpu.get_barrier_semaphore()
    near = [sibling]
    near += [at_y(k) for k in range(1, NY)]
    near += [at_z(k) for k in range(1, NZ)]
    near += [at_x(k) for k in range(1, NX)]
    for device in near:
        pl.semaphore_signal(barrier, inc=1, device_id=device, device_id_type=MESH)

    weights = {}
    for number, (src, dst) in enumerate(((gate, gate_v), (up, up_v), (down, down_v))):
        for at in (3, 0, 1, 2):
            made = pltpu.make_async_copy(
                src.at[:, pl.ds(at * FB, FB)], dst.at[at], wsem.at[number * NX + at]
            )
            made.start()
            weights[number, at] = made

    lane = iota((INFO, TOK), 0)
    dense = jnp.zeros((INFO, TOK), F32)
    for k in range(routes.shape[0]):
        dense = dense + jnp.where(routes[k : k + 1, :] == lane % 64, probs[k : k + 1, :], 0.0)
    high = dense.astype(BF).astype(F32)
    info = jnp.where(lane < 64, high, dense - high)
    got[y, z, c, :, :INFO] = info.T.astype(BF)
    got[y, z, c, :, INFO:] = tokens[...]

    pl.semaphore_wait(barrier, len(near))

    def prune():
        weights[0, 3].wait()
        w_t[...] = gate_v[3, :, FB - PANEL :].astype(F32).T
        drop_t[...] = (1 - masks[...]).astype(F32).T
        eye = iota((PANEL, PANEL), 0) == iota((PANEL, PANEL), 1)
        upper = factor[...]
        diagonal = jnp.sum(jnp.where(eye, upper, 0.0), axis=1, keepdims=True)
        v_t[...] = (upper / diagonal).T
        err_t[...] = jnp.zeros_like(err_t)
        yield
        for block in range(PANEL // 16):
            lo, hi = block * 16, block * 16 + 16
            seg = w_t[lo:hi, :]
            if block:
                seg = seg - jnp.dot(
                    v_t[lo:hi, :], err_t[...], precision=lax.Precision.HIGHEST, preferred_element_type=F32
                )
            near_t = v_t[lo:hi, lo:hi]
            drop = drop_t[lo:hi, :]
            errors = []
            for i in range(16):
                error = seg[i : i + 1, :] * drop[i : i + 1, :]
                errors.append(error)
                seg = seg - near_t[:, i : i + 1] * error
            err_t[lo:hi, :] = jnp.concatenate(errors, axis=0)
            w_t[lo:hi, :] = seg * (1.0 - drop)
            yield
        result = w_t[...].T.astype(BF)
        pruned_out[...] = result
        gate_v[3, :, FB - PANEL :] = result
        at = iota((PANEL, FB), 1) - (z * NC + c) * BLK
        unit[...] = jnp.where((at == iota((PANEL, FB), 0)) & (at < BLK), 1.0, 0.0).astype(BF)

    pruning = prune()

    def tick(times):
        for _ in range(times):
            next(pruning, None)

    def cut(ref, h):
        return ref.at[:, pl.ds(CUTS[h][0], CUTS[h][1])]

    along_z, along_y, shared = {}, {}, {}
    for h in range(2):
        block = cut(got.at[y, z, c], h)
        for k in ZNEAR:
            along_z[h, k] = net.copy(block, block, at_z(k))
        for m in YNEAR:
            along_y[h, 0, m] = net.copy(block, block, at_y(m))
    tick(3)

    before = (iota((CT, CT), 0) // TOK == iota((CT, CT), 1) // TOK) & (iota((CT, CT), 0) < iota((CT, CT), 1))
    before = before.astype(F32).astype(BF)
    slot_i, tok_i = iota((CH, CT), 0), iota((CH, CT), 1)
    pick = iota((8, INFO), 1)
    pick = jnp.where((pick == expert) | (pick == expert + 64), 1.0, 0.0).astype(BF)

    def choose(j):
        prob = lax.dot_general(
            pick, got[j, :, :, :, :INFO].reshape(CT, INFO), CONTRACT, preferred_element_type=F32
        )
        rank = jnp.dot((prob > 0.0).astype(F32).astype(BF), before, preferred_element_type=F32)
        chosen = (
            (slot_i // CAP == tok_i // TOK)
            & (rank[0:1, :] == (slot_i % CAP).astype(F32))
            & (prob[0:1, :] > 0.0)
        )
        chosen = jnp.where(chosen, 1.0, 0.0)
        slot_prob[j] = jnp.sum(chosen * prob[0:1, :], axis=1, keepdims=True)
        sel[j] = chosen

    ring = {}

    def launch(m, h):
        j = wrap(y - m, NY)
        shared[m, h].wait_recv()
        if h == 0:
            choose(j)
        start, width = CUTS[h][0] + (INFO if h == 0 else 0), HALF
        rows[x, h, j] = jnp.dot(
            sel[j].astype(BF),
            got[j, :, :, :, start : start + width].reshape(CT, width),
            preferred_element_type=F32,
        ).astype(BF)
        block = rows.at[x, h, j]
        ring[m, h, 0] = net.copy(block, block, at_x(d))
        ring[m, h, 1] = net.copy(block, block, at_x(-d))

    def relay(m, h):
        j = wrap(y - m, NY)
        ring[m, h, 0].wait_recv()
        block = rows.at[wrap(x - d, NX), h, j]
        ring[m, h, 2] = net.copy(block, block, at_x(d))

    def share(m, h):
        ref = got.at[wrap(y - m, NY), :, c, :, pl.ds(CUTS[h][0], CUTS[h][1])]
        shared[m, h] = net.copy(ref, ref, sibling)

    def forward(h, ks):
        for k in ks:
            along_z[h, k].wait_recv()
            block = cut(got.at[y, wrap(z - k, NZ), c], h)
            for m in YNEAR:
                along_y[h, k, m] = net.copy(block, block, at_y(m))

    def arrive(m, h):
        for k in (0,) + ZNEAR if m != 2 else (0,):
            along_y[h, k, m].wait_recv()
        if m == (1, 3)[h]:
            ref = got.at[wrap(y - m, NY), :, c, :, pl.ds(CUTS[h][0], CUTS[h][1])]
            along_y[h, 0, 2] = net.copy(ref, ref, at_y(m))
        share(m, h)

    forward(0, ZNEAR)
    share(0, 0)
    tick(1)
    forward(1, ZNEAR[:2])
    launch(0, 0)
    forward(1, ZNEAR[2:])
    share(0, 1)
    tick(1)
    launch(0, 1)
    relay(0, 0)
    order = [(0, 0), (0, 1), (1, 0), (3, 0), (3, 1), (1, 1), (2, 0), (2, 1)]
    arrive(*order[2])
    for n in range(2, len(order)):
        tick(1)
        if n < len(order) - 1:
            arrive(*order[n + 1])
        launch(*order[n])
        relay(*order[n - 1])
    relay(*order[-1])
    tick(16)

    for key in sorted(weights):
        if key != (0, 3):
            weights[key].wait()

    def project(o, h):
        block = rows[o, h].reshape(SLOTS, HALF)
        at = slice(h * HALF, (h + 1) * HALF)
        return (
            lax.dot_general(block, gate_v[o, :, at], CONTRACT, preferred_element_type=F32),
            lax.dot_general(block, up_v[o, :, at], CONTRACT, preferred_element_type=F32),
        )

    gate_val, up_val = project(x, 0)
    for hop, o in ((None, x), (1, wrap(x + d, NX)), (0, wrap(x - d, NX)), (2, wrap(x + 2, NX))):
        for h in range(2):
            if hop is None and h == 0:
                continue
            if hop in (1, 2):
                for m in PLANES:
                    ring[m, h, hop].wait_recv()
            more = project(o, h)
            gate_val, up_val = gate_val + more[0], up_val + more[1]
    hidden = (gate_val / (1.0 + jnp.exp(-gate_val)) * up_val).astype(BF)

    def partial(o):
        part[o] = jnp.dot(hidden, down_v[o], preferred_element_type=F32).astype(BF).reshape(NY, CH, FB)

    steps = (2, 1, 3, 0)
    planes = [wrap(y + k, NY) for k in steps]
    sums, back, along, across = {}, {}, {}, {}

    def place(n):
        h = n // NY
        return planes[n % NY], pl.ds(BASE[h], RET[h]), pl.ds(0, RET[h])

    def first(n):
        j, at, to = place(n)
        sums[n, 0] = net.copy(part.at[wrap(x + 2, NX), j, :, at], land.at[n, 0, :, to], at_x(d))

    def other(n):
        j, at, to = place(n)
        sums[n, 1] = net.copy(part.at[wrap(x - d, NX), j, :, at], land.at[n, 1, :, to], at_x(-d))

    def second(n):
        j, at, to = place(n)
        sums[n, 0].wait_recv()
        turn[n, :, to] = (land[n, 0, :, to].astype(F32) + part[wrap(x + d, NX), j, :, at].astype(F32)).astype(BF)
        sums[n, 2] = net.copy(turn.at[n, :, to], land.at[n, 2, :, to], at_x(d))

    def finish(n):
        j, at, to = place(n)
        sums[n, 1].wait_recv()
        sums[n, 2].wait_recv()
        total = part[x, j, :, at].astype(F32) + land[n, 1, :, to].astype(F32) + land[n, 2, :, to].astype(F32)
        scaled = (total * slot_prob[j]).astype(BF)
        spread[n, :, :, :, to] = (
            jnp.dot(sel[j].T.astype(BF), scaled, preferred_element_type=F32)
            .astype(BF)
            .reshape(NZ, NC, TOK, RET[n // NY])
        )
        back[n] = net.copy(spread.at[n, :, 1 - c, :, to], sib.at[n, :, :, to], sibling)

    def onward(n):
        back[n].wait_recv()
        h, k = n // NY, n % NY
        to = pl.ds(0, RET[h])
        total = spread[n, :, c, :, to].astype(F32) + sib[n, :, :, to].astype(F32)
        if k < NY - 1:
            slot = h * (NY - 1) + k
            ysend[slot, :, :, to] = total.astype(BF)
            along[h, k] = net.copy(ysend.at[slot, :, :, to], yland.at[slot, :, :, to], at_y(steps[k]))
        else:
            own[h, :, :, to] = total

    def whole(h, i):
        to = pl.ds(0, RET[h])
        total = own[h, i, :, to]
        for k in range(NY - 1):
            total = total + yland[h * (NY - 1) + k, i, :, to].astype(F32)
        return total

    def cross(h):
        for k in range(NY - 1):
            along[h, k].wait_recv()
        for k in ZNEAR:
            slot = h * (NZ - 1) + k - 1
            to = pl.ds(0, RET[h])
            zsend[slot, :, to] = whole(h, wrap(z + k, NZ)).astype(BF)
            across[h, k] = net.copy(zsend.at[slot, :, to], zland.at[slot, :, to], at_z(k))

    def settle(h):
        result = whole(h, z)
        for k in ZNEAR:
            across[h, k].wait_recv()
            result = result + zland[h * (NZ - 1) + k - 1, :, pl.ds(0, RET[h])].astype(F32)
        result = result.astype(BF)
        moe_out[:, pl.ds(BASE[h], RET[h])] = result
        full[y, z, c, :, pl.ds(BASE[h], RET[h])] = result

    cuts = (pl.ds(0, RET[0]), pl.ds(RET[0], WA))
    tail = pl.ds(RET[0] + WA, WB)
    az, ay, by, bz, sa = {}, {}, {}, {}, {}

    def spread_z(h):
        ref = full.at[y, z, c, :, cuts[h]]
        for k in ZNEAR:
            az[h, k] = net.copy(ref, ref, at_z(k))
        for m in HOPS[h]:
            ay[h, 0, m] = net.copy(ref, ref, at_y(m))

    def spread_y(h, ks):
        for k in ks:
            az[h, k].wait_recv()
            ref = full.at[y, wrap(z - k, NZ), c, :, cuts[h]]
            for m in HOPS[h]:
                ay[h, k, m] = net.copy(ref, ref, at_y(m))

    def draw(j, h):
        at = pl.ds(BASE[h], RET[h])
        more = lax.dot_general(
            unit[:, at], full[j, :, :, :, at].reshape(CT, RET[h]), CONTRACT, preferred_element_type=F32
        ).astype(BF)
        right[j] = more if h == 0 else right[j] + more

    def share_own(h):
        ref = full.at[y, :, c, :, cuts[h]]
        sa[h, 0] = net.copy(ref, ref, sibling)

    def collect(h, m):
        for k in (0,) + ZNEAR if m in HOPS[h] else (0,):
            ay[h, k, m].wait_recv()
        ref = full.at[wrap(y - m, NY), :, c, :, cuts[h]]
        sa[h, m] = net.copy(ref, ref, sibling)

    partial(wrap(x + 2, NX))
    for n in range(2):
        first(n)
    partial(wrap(x - d, NX))
    for n in range(2):
        other(n)
    partial(wrap(x + d, NX))
    partial(x)
    for n in range(2 * NY):
        second(n)
        if n + 2 < 2 * NY:
            first(n + 2)
            other(n + 2)
        if n >= 1:
            finish(n - 1)
        if n >= 2:
            onward(n - 2)
    cross(0)
    finish(7)
    onward(6)
    onward(7)
    settle(0)
    spread_z(0)
    cross(1)
    spread_y(0, ZNEAR)
    share_own(0)
    settle(1)
    ref = full.at[y, z, c, :, tail]
    for m in (1, 2, 3):
        by[m] = net.copy(ref, ref, at_y(m))
    spread_z(1)
    spread_y(1, ZNEAR[:2])
    for m in (1, 2, 3):
        by[m].wait_recv()
    ref = full.at[:, z, c, :, tail]
    for k in ZNEAR:
        bz[k] = net.copy(ref, ref, at_z(k))
    spread_y(1, ZNEAR[2:])
    share_own(1)
    for m in PLANES:
        if m:
            collect(0, m)
        sa[0, m].wait_recv()
        pl.when(x == y)(functools.partial(draw, wrap(y - m, NY), 0))
    for k in ZNEAR:
        bz[k].wait_recv()
    ref = full.at[:, :, c, :, tail]
    sb = net.copy(ref, ref, sibling)
    sb.wait_recv()

    scale = 2.0 / (TOK * NY * NZ * NC)
    cols = {}

    def product(n):
        j = wrap(y - PLANES[n], NY)

        @pl.when(x != y)
        def _():
            cols[n][0].wait_recv()

        for at in range(0, FB, 256):
            more = jnp.dot(
                right[j], full[j, :, :, :, at : at + 256].reshape(CT, 256), preferred_element_type=F32
            )
            if n == 0:
                acc[:, at : at + 256] = more
            elif n < NY - 1:
                acc[:, at : at + 256] += more
            else:
                hess_out[:, at : at + 256] = ((acc[:, at : at + 256] + more) * scale)[:BLK, :]

    for n, m in enumerate(PLANES):
        j = wrap(y - m, NY)
        if m:
            collect(1, m)
        sa[1, m].wait_recv()
        index = net.count
        cols[n] = [net.make(right.at[j], right.at[j], at_x(k), index) for k in (2, 1, 3)]

        @pl.when(x == y)
        def _():
            draw(j, 1)
            for made in cols[n]:
                made.start()

        if n:
            product(n - 1)
    product(NY - 1)

    @pl.when(x == y)
    def _():
        for n in range(NY):
            for made in cols[n]:
                made.wait_send()

    net.drain()


def hand_on(pruned, moe, hessian, pruned_out, moe_out, hess_out):
    pruned_out[...] = pruned[...]
    moe_out[...] = moe[...]
    hess_out[...] = hessian[...]


def on_device(tokens, routes, probs, gate_weight, up_weight, down_weight, masks, inv_factor):
    vmem = pl.BlockSpec(memory_space=pltpu.VMEM)
    hbm = pl.BlockSpec(memory_space=pl.ANY)
    scratch = [
        pltpu.VMEM((NX, HID, FB), BF),
        pltpu.VMEM((NX, HID, FB), BF),
        pltpu.VMEM((NX, HID, FB), BF),
        pltpu.VMEM((NY, NZ, NC, TOK, WIDE), BF),
        pltpu.VMEM((NX, 2, NY, CH, HALF), BF),
        pltpu.VMEM((NY, CH, CT), F32),
        pltpu.VMEM((NY, CH, 1), F32),
        pltpu.VMEM((NX, NY, CH, FB), BF),
        pltpu.VMEM((2 * NY, CH, RET[0]), BF),
        pltpu.VMEM((2 * NY, 3, CH, RET[0]), BF),
        pltpu.VMEM((2 * NY, NZ, NC, TOK, RET[0]), BF),
        pltpu.VMEM((2 * NY, NZ, TOK, RET[0]), BF),
        pltpu.VMEM((2 * NY - 2, NZ, TOK, RET[0]), BF),
        pltpu.VMEM((2 * NY - 2, NZ, TOK, RET[0]), BF),
        pltpu.VMEM((2, NZ, TOK, RET[0]), F32),
        pltpu.VMEM((2 * NZ - 2, TOK, RET[0]), BF),
        pltpu.VMEM((2 * NZ - 2, TOK, RET[0]), BF),
        pltpu.VMEM((NY, NZ, NC, TOK, FB), BF),
        pltpu.VMEM((PANEL, FB), BF),
        pltpu.VMEM((NY, PANEL, CT), BF),
        pltpu.VMEM((PANEL, FB), F32),
        pltpu.VMEM((PANEL, HID), F32),
        pltpu.VMEM((PANEL, HID), F32),
        pltpu.VMEM((PANEL, PANEL), F32),
        pltpu.VMEM((PANEL, HID), F32),
        pltpu.SemaphoreType.DMA((12,)),
        pltpu.SemaphoreType.DMA((COPIES,)),
        pltpu.SemaphoreType.DMA((COPIES,)),
    ]
    shapes = (
        jax.ShapeDtypeStruct((HID, PANEL), BF),
        jax.ShapeDtypeStruct((TOK, FB), BF),
        jax.ShapeDtypeStruct((BLK, FB), F32),
    )
    results = pl.pallas_call(
        body,
        out_shape=shapes,
        in_specs=[vmem, vmem, vmem, hbm, hbm, hbm, vmem, vmem],
        out_specs=(vmem, vmem, vmem),
        scratch_shapes=scratch,
        compiler_params=pltpu.CompilerParams(
            collective_id=0, has_side_effects=True, vmem_limit_bytes=58 * 1024 * 1024
        ),
        cost_estimate=pl.CostEstimate(flops=6_000_000_000, bytes_accessed=14_000_000, transcendentals=65536),
        name="expert_layer",
    )(tokens, routes.T, probs.T, gate_weight[0], up_weight[0], down_weight[0], masks[0], inv_factor)
    pruned, moe, hessian = pl.pallas_call(
        hand_on,
        out_shape=shapes,
        in_specs=[vmem, vmem, vmem],
        out_specs=(vmem, vmem, vmem),
        name="hand_on",
    )(*results)
    return pruned[None], moe, hessian.T


def solution(mesh):
    in_specs = (
        P("expert", "row"),
        P("expert", None),
        P("expert", None),
        P("expert", "row", None),
        P("expert", "row", None),
        P("expert", "row", None),
        P("expert", "row", None),
        P(),
    )
    out_specs = (P("expert", "row", None), P("expert", "row"), P("row", "expert"))
    return jax.shard_map(
        on_device, mesh=mesh, in_specs=in_specs, out_specs=out_specs, check_vma=False
    )
```

```python
import functools

import jax
import jax.numpy as jnp
from jax import lax
from jax.experimental import pallas as pl
from jax.experimental.pallas import tpu as pltpu
from jax.sharding import PartitionSpec as P

NX, NY, NZ, NC = 4, 4, 8, 2
TOK = 16
CAP = 4
PANEL = 128
FB = 1792
HALF = FB // 2
INFO = 128
WIDE = INFO + FB
CUTS = ((0, INFO + HALF), (INFO + HALF, HALF))
RET = (896, FB - 896)
BASE = (0, RET[0])
WB = 128
WA = RET[1] - WB
SLOTS = CAP * NY * NZ * NC
CH = SLOTS // NY
HID = 256
CT = NZ * NC * TOK
BLK = 112
MESH = pl.DeviceIdType.MESH
F32 = jnp.float32
BF = jnp.bfloat16
COPIES = 240
CONTRACT = (((1,), (1,)), ((), ()))
ZNEAR = (1, 7, 2, 6, 3, 5, 4)
YNEAR = (1, 3)
HOPS = ((1, 3, 2), (1, 3, 2))
PLANES = (0, 1, 3, 2)


def wrap(value, n):
    return lax.rem(value + 4 * n, n)


def iota(shape, axis):
    return lax.broadcasted_iota(jnp.int32, shape, axis)


class Net:
    def __init__(self, send, recv):
        self.send, self.recv, self.count, self.pending = send, recv, 0, []

    def make(self, src, dst, dev, recv_index=None):
        index = self.count
        self.count += 1
        return pltpu.make_async_remote_copy(
            src_ref=src,
            dst_ref=dst,
            send_sem=self.send.at[index],
            recv_sem=self.recv.at[index if recv_index is None else recv_index],
            device_id=dev,
            device_id_type=MESH,
        )

    def copy(self, src, dst, dev):
        made = self.make(src, dst, dev)
        made.start()
        self.pending.append(made)
        return made

    def drain(self):
        for made in self.pending:
            made.wait_send()


def body(
    tokens, routes, probs, gate, up, down, masks, factor,
    pruned_out, moe_out, hess_out,
    gate_v, up_v, down_v, got, rows, sel, slot_prob, part, turn, land,
    spread, sib, ysend, yland, own, zsend, zland,
    full, unit, right, acc, w_t, drop_t, v_t, err_t, wsem, send, recv,
):
    expert = lax.axis_index("expert")
    x = lax.axis_index("row")
    y, z, c = expert // (NZ * NC), (expert // NC) % NZ, expert % NC
    d = 1 - 2 * c
    net = Net(send, recv)

    def at_y(k):
        return ((wrap(y + k, NY) * NZ + z) * NC + c, x)

    def at_z(k):
        return ((y * NZ + wrap(z + k, NZ)) * NC + c, x)

    def at_x(k):
        return (expert, wrap(x + k, NX))

    sibling = (expert + d, x)

    barrier = pltpu.get_barrier_semaphore()
    near = [sibling]
    near += [at_y(k) for k in range(1, NY)]
    near += [at_z(k) for k in range(1, NZ)]
    near += [at_x(k) for k in range(1, NX)]
    for device in near:
        pl.semaphore_signal(barrier, inc=1, device_id=device, device_id_type=MESH)

    weights = {}
    for number, (src, dst) in enumerate(((gate, gate_v), (up, up_v), (down, down_v))):
        for at in (3, 0, 1, 2):
            made = pltpu.make_async_copy(
                src.at[:, pl.ds(at * FB, FB)], dst.at[at], wsem.at[number * NX + at]
            )
            made.start()
            weights[number, at] = made

    lane = iota((INFO, TOK), 0)
    dense = jnp.zeros((INFO, TOK), F32)
    for k in range(routes.shape[0]):
        dense = dense + jnp.where(routes[k : k + 1, :] == lane % 64, probs[k : k + 1, :], 0.0)
    high = dense.astype(BF).astype(F32)
    info = jnp.where(lane < 64, high, dense - high)
    got[y, z, c, :, :INFO] = info.T.astype(BF)
    got[y, z, c, :, INFO:] = tokens[...]

    pl.semaphore_wait(barrier, len(near))

    def prune():
        weights[0, 3].wait()
        w_t[...] = gate_v[3, :, FB - PANEL :].astype(F32).T
        drop_t[...] = (1 - masks[...]).astype(F32).T
        eye = iota((PANEL, PANEL), 0) == iota((PANEL, PANEL), 1)
        upper = factor[...]
        diagonal = jnp.sum(jnp.where(eye, upper, 0.0), axis=1, keepdims=True)
        v_t[...] = (upper / diagonal).T
        err_t[...] = jnp.zeros_like(err_t)
        yield
        for block in range(PANEL // 16):
            lo, hi = block * 16, block * 16 + 16
            seg = w_t[lo:hi, :]
            if block:
                seg = seg - jnp.dot(
                    v_t[lo:hi, :], err_t[...], precision=lax.Precision.HIGHEST, preferred_element_type=F32
                )
            near_t = v_t[lo:hi, lo:hi]
            drop = drop_t[lo:hi, :]
            errors = []
            for i in range(16):
                error = seg[i : i + 1, :] * drop[i : i + 1, :]
                errors.append(error)
                seg = seg - near_t[:, i : i + 1] * error
            err_t[lo:hi, :] = jnp.concatenate(errors, axis=0)
            w_t[lo:hi, :] = seg * (1.0 - drop)
            yield
        result = w_t[...].T.astype(BF)
        pruned_out[...] = result
        gate_v[3, :, FB - PANEL :] = result
        at = iota((PANEL, FB), 1) - (z * NC + c) * BLK
        unit[...] = jnp.where((at == iota((PANEL, FB), 0)) & (at < BLK), 1.0, 0.0).astype(BF)

    pruning = prune()

    def tick(times):
        for _ in range(times):
            next(pruning, None)

    def cut(ref, h):
        return ref.at[:, pl.ds(CUTS[h][0], CUTS[h][1])]

    along_z, along_y, shared = {}, {}, {}
    for h in range(2):
        block = cut(got.at[y, z, c], h)
        for k in ZNEAR:
            along_z[h, k] = net.copy(block, block, at_z(k))
        for m in YNEAR:
            along_y[h, 0, m] = net.copy(block, block, at_y(m))
    tick(3)

    before = (iota((CT, CT), 0) // TOK == iota((CT, CT), 1) // TOK) & (iota((CT, CT), 0) < iota((CT, CT), 1))
    before = before.astype(F32).astype(BF)
    slot_i, tok_i = iota((CH, CT), 0), iota((CH, CT), 1)
    pick = iota((8, INFO), 1)
    pick = jnp.where((pick == expert) | (pick == expert + 64), 1.0, 0.0).astype(BF)

    def choose(j):
        prob = lax.dot_general(
            pick, got[j, :, :, :, :INFO].reshape(CT, INFO), CONTRACT, preferred_element_type=F32
        )
        rank = jnp.dot((prob > 0.0).astype(F32).astype(BF), before, preferred_element_type=F32)
        chosen = (
            (slot_i // CAP == tok_i // TOK)
            & (rank[0:1, :] == (slot_i % CAP).astype(F32))
            & (prob[0:1, :] > 0.0)
        )
        chosen = jnp.where(chosen, 1.0, 0.0)
        slot_prob[j] = jnp.sum(chosen * prob[0:1, :], axis=1, keepdims=True)
        sel[j] = chosen

    ring = {}

    def launch(m, h):
        j = wrap(y - m, NY)
        shared[m, h].wait_recv()
        if h == 0:
            choose(j)
        start, width = CUTS[h][0] + (INFO if h == 0 else 0), HALF
        rows[x, h, j] = jnp.dot(
            sel[j].astype(BF),
            got[j, :, :, :, start : start + width].reshape(CT, width),
            preferred_element_type=F32,
        ).astype(BF)
        block = rows.at[x, h, j]
        ring[m, h, 0] = net.copy(block, block, at_x(d))
        ring[m, h, 1] = net.copy(block, block, at_x(-d))

    def relay(m, h):
        j = wrap(y - m, NY)
        ring[m, h, 0].wait_recv()
        block = rows.at[wrap(x - d, NX), h, j]
        ring[m, h, 2] = net.copy(block, block, at_x(d))

    def share(m, h):
        ref = got.at[wrap(y - m, NY), :, c, :, pl.ds(CUTS[h][0], CUTS[h][1])]
        shared[m, h] = net.copy(ref, ref, sibling)

    def forward(h, ks):
        for k in ks:
            along_z[h, k].wait_recv()
            block = cut(got.at[y, wrap(z - k, NZ), c], h)
            for m in YNEAR:
                along_y[h, k, m] = net.copy(block, block, at_y(m))

    def arrive(m, h):
        for k in (0,) + ZNEAR if m != 2 else (0,):
            along_y[h, k, m].wait_recv()
        if m == (1, 3)[h]:
            ref = got.at[wrap(y - m, NY), :, c, :, pl.ds(CUTS[h][0], CUTS[h][1])]
            along_y[h, 0, 2] = net.copy(ref, ref, at_y(m))
        share(m, h)

    forward(0, ZNEAR)
    share(0, 0)
    tick(1)
    forward(1, ZNEAR[:2])
    launch(0, 0)
    forward(1, ZNEAR[2:])
    share(0, 1)
    tick(1)
    launch(0, 1)
    relay(0, 0)
    order = [(0, 0), (0, 1), (1, 0), (3, 0), (3, 1), (1, 1), (2, 0), (2, 1)]
    arrive(*order[2])
    for n in range(2, len(order)):
        tick(1)
        if n < len(order) - 1:
            arrive(*order[n + 1])
        launch(*order[n])
        if n > 2:
            relay(*order[n - 2])
    relay(*order[-2])
    relay(*order[-1])
    tick(16)

    for key in sorted(weights):
        if key != (0, 3):
            weights[key].wait()

    def project(o, h):
        block = rows[o, h].reshape(SLOTS, HALF)
        at = slice(h * HALF, (h + 1) * HALF)
        return (
            lax.dot_general(block, gate_v[o, :, at], CONTRACT, preferred_element_type=F32),
            lax.dot_general(block, up_v[o, :, at], CONTRACT, preferred_element_type=F32),
        )

    gate_val, up_val = project(x, 0)
    for hop, o in ((None, x), (1, wrap(x + d, NX)), (0, wrap(x - d, NX)), (2, wrap(x + 2, NX))):
        for h in range(2):
            if hop is None and h == 0:
                continue
            if hop in (1, 2):
                for m in PLANES:
                    ring[m, h, hop].wait_recv()
            more = project(o, h)
            gate_val, up_val = gate_val + more[0], up_val + more[1]
    hidden = (gate_val / (1.0 + jnp.exp(-gate_val)) * up_val).astype(BF)

    def partial(o):
        part[o] = jnp.dot(hidden, down_v[o], preferred_element_type=F32).astype(BF).reshape(NY, CH, FB)

    steps = (2, 1, 3, 0)
    planes = [wrap(y + k, NY) for k in steps]
    sums, back, along, across = {}, {}, {}, {}

    def place(n):
        h = n // NY
        return planes[n % NY], pl.ds(BASE[h], RET[h]), pl.ds(0, RET[h])

    def first(n):
        j, at, to = place(n)
        sums[n, 0] = net.copy(part.at[wrap(x + 2, NX), j, :, at], land.at[n, 0, :, to], at_x(d))

    def other(n):
        j, at, to = place(n)
        sums[n, 1] = net.copy(part.at[wrap(x - d, NX), j, :, at], land.at[n, 1, :, to], at_x(-d))

    def second(n):
        j, at, to = place(n)
        sums[n, 0].wait_recv()
        turn[n, :, to] = (land[n, 0, :, to].astype(F32) + part[wrap(x + d, NX), j, :, at].astype(F32)).astype(BF)
        sums[n, 2] = net.copy(turn.at[n, :, to], land.at[n, 2, :, to], at_x(d))

    def finish(n):
        j, at, to = place(n)
        sums[n, 1].wait_recv()
        sums[n, 2].wait_recv()
        total = part[x, j, :, at].astype(F32) + land[n, 1, :, to].astype(F32) + land[n, 2, :, to].astype(F32)
        scaled = (total * slot_prob[j]).astype(BF)
        spread[n, :, :, :, to] = (
            jnp.dot(sel[j].T.astype(BF), scaled, preferred_element_type=F32)
            .astype(BF)
            .reshape(NZ, NC, TOK, RET[n // NY])
        )
        back[n] = net.copy(spread.at[n, :, 1 - c, :, to], sib.at[n, :, :, to], sibling)

    def onward(n):
        back[n].wait_recv()
        h, k = n // NY, n % NY
        to = pl.ds(0, RET[h])
        total = spread[n, :, c, :, to].astype(F32) + sib[n, :, :, to].astype(F32)
        if k < NY - 1:
            slot = h * (NY - 1) + k
            ysend[slot, :, :, to] = total.astype(BF)
            along[h, k] = net.copy(ysend.at[slot, :, :, to], yland.at[slot, :, :, to], at_y(steps[k]))
        else:
            own[h, :, :, to] = total

    def whole(h, i):
        to = pl.ds(0, RET[h])
        total = own[h, i, :, to]
        for k in range(NY - 1):
            total = total + yland[h * (NY - 1) + k, i, :, to].astype(F32)
        return total

    def cross(h):
        for k in range(NY - 1):
            along[h, k].wait_recv()
        for k in ZNEAR:
            slot = h * (NZ - 1) + k - 1
            to = pl.ds(0, RET[h])
            zsend[slot, :, to] = whole(h, wrap(z + k, NZ)).astype(BF)
            across[h, k] = net.copy(zsend.at[slot, :, to], zland.at[slot, :, to], at_z(k))

    def settle(h):
        result = whole(h, z)
        for k in ZNEAR:
            across[h, k].wait_recv()
            result = result + zland[h * (NZ - 1) + k - 1, :, pl.ds(0, RET[h])].astype(F32)
        result = result.astype(BF)
        moe_out[:, pl.ds(BASE[h], RET[h])] = result
        full[y, z, c, :, pl.ds(BASE[h], RET[h])] = result

    cuts = (pl.ds(0, RET[0]), pl.ds(RET[0], WA))
    tail = pl.ds(RET[0] + WA, WB)
    az, ay, by, bz, sa = {}, {}, {}, {}, {}

    def spread_z(h):
        ref = full.at[y, z, c, :, cuts[h]]
        for k in ZNEAR:
            az[h, k] = net.copy(ref, ref, at_z(k))
        for m in HOPS[h]:
            ay[h, 0, m] = net.copy(ref, ref, at_y(m))

    def spread_y(h, ks):
        for k in ks:
            az[h, k].wait_recv()
            ref = full.at[y, wrap(z - k, NZ), c, :, cuts[h]]
            for m in HOPS[h]:
                ay[h, k, m] = net.copy(ref, ref, at_y(m))

    def draw(j, h):
        at = pl.ds(BASE[h], RET[h])
        more = lax.dot_general(
            unit[:, at], full[j, :, :, :, at].reshape(CT, RET[h]), CONTRACT, preferred_element_type=F32
        ).astype(BF)
        right[j] = more if h == 0 else right[j] + more

    def share_own(h):
        ref = full.at[y, :, c, :, cuts[h]]
        sa[h, 0] = net.copy(ref, ref, sibling)

    def collect(h, m):
        for k in (0,) + ZNEAR if m in HOPS[h] else (0,):
            ay[h, k, m].wait_recv()
        ref = full.at[wrap(y - m, NY), :, c, :, cuts[h]]
        sa[h, m] = net.copy(ref, ref, sibling)

    partial(wrap(x + 2, NX))
    for n in range(2):
        first(n)
    partial(wrap(x - d, NX))
    for n in range(2):
        other(n)
    partial(wrap(x + d, NX))
    partial(x)
    for n in range(2 * NY):
        second(n)
        if n + 2 < 2 * NY:
            first(n + 2)
            other(n + 2)
        if n == 2 * NY - 1:
            cross(0)
        if n >= 1:
            finish(n - 1)
        if n >= 2:
            onward(n - 2)
    onward(6)
    finish(7)
    onward(7)
    settle(0)
    spread_z(0)
    cross(1)
    spread_y(0, ZNEAR)
    share_own(0)
    settle(1)
    ref = full.at[y, z, c, :, tail]
    for m in (1, 2, 3):
        by[m] = net.copy(ref, ref, at_y(m))
    spread_z(1)
    spread_y(1, ZNEAR[:2])
    for m in (1, 2, 3):
        by[m].wait_recv()
    ref = full.at[:, z, c, :, tail]
    for k in ZNEAR:
        bz[k] = net.copy(ref, ref, at_z(k))
    spread_y(1, ZNEAR[2:])
    share_own(1)
    for m in PLANES:
        if m:
            collect(0, m)
        sa[0, m].wait_recv()
        pl.when(x == y)(functools.partial(draw, wrap(y - m, NY), 0))
    for k in ZNEAR:
        bz[k].wait_recv()
    ref = full.at[:, :, c, :, tail]
    sb = net.copy(ref, ref, sibling)
    sb.wait_recv()

    scale = 2.0 / (TOK * NY * NZ * NC)
    cols = {}

    def product(n):
        j = wrap(y - PLANES[n], NY)

        @pl.when(x != y)
        def _():
            cols[n][0].wait_recv()

        for at in range(0, FB, 256):
            more = jnp.dot(
                right[j], full[j, :, :, :, at : at + 256].reshape(CT, 256), preferred_element_type=F32
            )
            if n == 0:
                acc[:, at : at + 256] = more
            elif n < NY - 1:
                acc[:, at : at + 256] += more
            else:
                hess_out[:, at : at + 256] = ((acc[:, at : at + 256] + more) * scale)[:BLK, :]

    for n, m in enumerate(PLANES):
        j = wrap(y - m, NY)
        if m:
            collect(1, m)
        sa[1, m].wait_recv()
        index = net.count
        cols[n] = [net.make(right.at[j], right.at[j], at_x(k), index) for k in (2, 1, 3)]

        @pl.when(x == y)
        def _():
            draw(j, 1)
            for made in cols[n]:
                made.start()

        if n:
            product(n - 1)
    product(NY - 1)

    @pl.when(x == y)
    def _():
        for n in range(NY):
            for made in cols[n]:
                made.wait_send()

    net.drain()


def hand_on(pruned, moe, hessian, pruned_out, moe_out, hess_out):
    pruned_out[...] = pruned[...]
    moe_out[...] = moe[...]
    hess_out[...] = hessian[...]


def on_device(tokens, routes, probs, gate_weight, up_weight, down_weight, masks, inv_factor):
    vmem = pl.BlockSpec(memory_space=pltpu.VMEM)
    hbm = pl.BlockSpec(memory_space=pl.ANY)
    scratch = [
        pltpu.VMEM((NX, HID, FB), BF),
        pltpu.VMEM((NX, HID, FB), BF),
        pltpu.VMEM((NX, HID, FB), BF),
        pltpu.VMEM((NY, NZ, NC, TOK, WIDE), BF),
        pltpu.VMEM((NX, 2, NY, CH, HALF), BF),
        pltpu.VMEM((NY, CH, CT), F32),
        pltpu.VMEM((NY, CH, 1), F32),
        pltpu.VMEM((NX, NY, CH, FB), BF),
        pltpu.VMEM((2 * NY, CH, RET[0]), BF),
        pltpu.VMEM((2 * NY, 3, CH, RET[0]), BF),
        pltpu.VMEM((2 * NY, NZ, NC, TOK, RET[0]), BF),
        pltpu.VMEM((2 * NY, NZ, TOK, RET[0]), BF),
        pltpu.VMEM((2 * NY - 2, NZ, TOK, RET[0]), BF),
        pltpu.VMEM((2 * NY - 2, NZ, TOK, RET[0]), BF),
        pltpu.VMEM((2, NZ, TOK, RET[0]), F32),
        pltpu.VMEM((2 * NZ - 2, TOK, RET[0]), BF),
        pltpu.VMEM((2 * NZ - 2, TOK, RET[0]), BF),
        pltpu.VMEM((NY, NZ, NC, TOK, FB), BF),
        pltpu.VMEM((PANEL, FB), BF),
        pltpu.VMEM((NY, PANEL, CT), BF),
        pltpu.VMEM((PANEL, FB), F32),
        pltpu.VMEM((PANEL, HID), F32),
        pltpu.VMEM((PANEL, HID), F32),
        pltpu.VMEM((PANEL, PANEL), F32),
        pltpu.VMEM((PANEL, HID), F32),
        pltpu.SemaphoreType.DMA((12,)),
        pltpu.SemaphoreType.DMA((COPIES,)),
        pltpu.SemaphoreType.DMA((COPIES,)),
    ]
    shapes = (
        jax.ShapeDtypeStruct((HID, PANEL), BF),
        jax.ShapeDtypeStruct((TOK, FB), BF),
        jax.ShapeDtypeStruct((BLK, FB), F32),
    )
    results = pl.pallas_call(
        body,
        out_shape=shapes,
        in_specs=[vmem, vmem, vmem, hbm, hbm, hbm, vmem, vmem],
        out_specs=(vmem, vmem, vmem),
        scratch_shapes=scratch,
        compiler_params=pltpu.CompilerParams(
            collective_id=0, has_side_effects=True, vmem_limit_bytes=58 * 1024 * 1024
        ),
        cost_estimate=pl.CostEstimate(flops=6_000_000_000, bytes_accessed=14_000_000, transcendentals=65536),
        name="expert_layer",
    )(tokens, routes.T, probs.T, gate_weight[0], up_weight[0], down_weight[0], masks[0], inv_factor)
    pruned, moe, hessian = pl.pallas_call(
        hand_on,
        out_shape=shapes,
        in_specs=[vmem, vmem, vmem],
        out_specs=(vmem, vmem, vmem),
        name="hand_on",
    )(*results)
    return pruned[None], moe, hessian.T


def solution(mesh):
    in_specs = (
        P("expert", "row"),
        P("expert", None),
        P("expert", None),
        P("expert", "row", None),
        P("expert", "row", None),
        P("expert", "row", None),
        P("expert", "row", None),
        P(),
    )
    out_specs = (P("expert", "row", None), P("expert", "row"), P("row", "expert"))
    return jax.shard_map(
        on_device, mesh=mesh, in_specs=in_specs, out_specs=out_specs, check_vma=False
    )
```
